256 devices in a mesh: grp: 8 (over x, core), node: 32 (over z, y).
Axes of the slice: x: 4, y: 4, z: 8, core: 2. Of those that a mesh axis runs over, the one named last changes fastest.
Arguments:
- samples: bfloat16 [131072, 512], P(('grp', 'node')), may hold values from -6 to 6
- omega: bfloat16 [131072, 512], P(('grp', 'node')), may hold values from -6 to 6
- diag_block: bfloat16 [131072, 512], P(('grp', 'node')), may hold values from -0.25 to 0.25
- leaf_pivots: int32 [256, 128], P(('grp', 'node')), may hold values from 0 to 511, as said below
- leaf_interp: bfloat16 [131072, 128], P(('grp', 'node')), may hold values from -0.25 to 0.25
- coupling: bfloat16 [32768, 128], P(('grp', 'node')), may hold values from -0.5 to 0.5
- parent_pivots: int32 [128, 128], P('grp'), may hold values from 0 to 255, as said below
- parent_interp: bfloat16 [32768, 128], P(('grp', 'node')), may hold values from -8 to 8
- far_coupling: bfloat16 [131072, 4096], P(('grp', 'node')), may hold values from -0.09375 to 0.09375
Outputs:
- parent_rows: bfloat16 [16384, 512], P(('grp', 'node'))
- transfer: bfloat16 [131072, 128], P(('grp', 'node'))
- far_field: bfloat16 [131072, 512], P(('grp', 'node'))
The draws below stay inside these ranges and needn't reach their ends.
Inputs may be any that keep to these rules, and one draw needn't show every extreme that they name: `leaf_pivots`: the 128 entries of a row are distinct local row numbers of the leaf. `parent_pivots`: the 128 entries of a row are distinct.
All inputs are finite; a program needn't handle non-finite values.
Results may differ from the reference program's by a relative error of at most 0.01.
Values may be sent and summed in bfloat16 or wider, within the bound.
No kernel may reach another device: no remote copies, remote signals or barrier semaphores. Data moves between devices by JAX's collectives and lax.ppermute only.
A program may use at most 64 MiB of HBM per device.

```python
import jax
import jax.numpy as jnp
from jax import lax

M = 512
K = 128
S = 512
N = 131072
GROUP_ROWS = 2048
PARENT_ROWS = 16384
N_GRP = 8
N_NODE = 32


def pick_distinct(key, row_count, value_count, pick_count):
    row_keys = jax.random.split(key, row_count)

    def pick_row(row_key):
        key_order, key_shuffle = jax.random.split(row_key)
        order = jax.random.permutation(key_order, value_count)
        where_top = jnp.argmax(order == value_count - 1)
        order = order.at[where_top].set(order[0]).at[0].set(value_count - 1)
        chosen = jax.random.permutation(key_shuffle, order[:pick_count])
        return chosen.astype(jnp.int32)
    return jax.vmap(pick_row)(row_keys)


def draw_leaf_pivots(key, part):
    return pick_distinct(jax.random.fold_in(key, 11), N_GRP * N_NODE, M, K)


def draw_parent_pivots(key, part):
    return pick_distinct(jax.random.fold_in(key, 23), N_GRP * N_NODE // 2, 2 * K, K)


def block_scale(stream_key, extent, cuts, low, largest):
    loudness, own = 1.0, jax.random.fold_in(stream_key, 6)
    for axis_at, parts in cuts:
        steps = jnp.exp(jax.random.uniform(jax.random.fold_in(own, axis_at), (parts,), jnp.float32, low / len(cuts), largest / len(cuts)))
        loudness = loudness * jnp.repeat(steps, extent[axis_at] // parts).reshape([-1 if axis == axis_at else 1 for axis in range(len(extent))])
    return loudness


def gaussian(stream_key, shape, width, most, cuts=(), dtype=jnp.bfloat16):
    level = block_scale(stream_key, shape, cuts, -0.22, 0.18) if cuts else 1.0
    values = jax.random.normal(stream_key, shape, jnp.float32) * width * level
    return jnp.minimum(jnp.maximum(values, -most), most).astype(dtype)


def setup_inputs(seed: int = 0) -> dict:
    splits = jax.random.split(jax.random.key(seed), 10)
    return {
        "samples": gaussian(splits[0], (N, S), 1.0, 6.0, ((0, 256),)),
        "omega": gaussian(splits[1], (N, S), 1.0, 6.0, ((0, 256),)),
        "diag_block": gaussian(splits[2], (N, M), M ** -0.5, 0.25, ((0, 256),)),
        "leaf_pivots": draw_leaf_pivots(jax.random.fold_in(splits[9], 71), 0),
        "leaf_interp": gaussian(splits[4], (N, K), M ** -0.5, 0.25, ((0, 256),)),
        "coupling": gaussian(splits[5], (N_GRP * N_NODE * K, K), K ** -0.5, 0.5, ((0, 256),)),
        "parent_pivots": draw_parent_pivots(jax.random.fold_in(splits[9], 71), 0),
        "parent_interp": gaussian(splits[7], (N_GRP * N_NODE * K, K), 2.0, 8.0, ((0, 256),)),
        "far_coupling": gaussian(splits[8], (N, 2 * GROUP_ROWS), (2 * GROUP_ROWS) ** -0.5, 0.09375, ((0, 256),)),
    }


def reference(samples, omega, diag_block, leaf_pivots, leaf_interp, coupling, parent_pivots, parent_interp, far_coupling):
    leaves = N_GRP * N_NODE
    sample_blocks = samples.reshape(leaves, M, S)
    omega_blocks = omega.reshape(leaves, M, S)
    diag_blocks = diag_block.reshape(leaves, M, M)
    picked_diag = jnp.take_along_axis(diag_blocks, leaf_pivots[:, :, None], axis=1)
    picked_rows = jnp.take_along_axis(sample_blocks, leaf_pivots[:, :, None], axis=1)
    skeleton = (picked_rows.astype(jnp.float32) - jnp.einsum("lkm,lms->lks", picked_diag.astype(jnp.float32), omega_blocks.astype(jnp.float32))).astype(jnp.bfloat16)
    interp_blocks = leaf_interp.reshape(leaves, M, K)
    compressed = jnp.einsum("lmk,lms->lks", interp_blocks.astype(jnp.float32), omega_blocks.astype(jnp.float32)).astype(jnp.bfloat16)
    sibling_basis = compressed.reshape(leaves // 2, 2, K, S)[:, ::-1].reshape(leaves, K, S)
    coupling_blocks = coupling.reshape(leaves, K, K)
    reduced = (skeleton.astype(jnp.float32) - jnp.einsum("lkj,ljs->lks", coupling_blocks.astype(jnp.float32), sibling_basis.astype(jnp.float32))).astype(jnp.bfloat16)
    merged = reduced.reshape(leaves // 2, 2 * K, S)
    parent = jnp.take_along_axis(merged, parent_pivots[:, :, None], axis=1)
    parent_rows = parent.reshape(PARENT_ROWS, S)
    parent_blocks = parent_interp.reshape(leaves, K, K)
    transfer = jnp.einsum("lmk,lkj->lmj", interp_blocks.astype(jnp.float32), parent_blocks.astype(jnp.float32)).astype(jnp.bfloat16).reshape(N, K)
    groups = parent.reshape(N_GRP, GROUP_ROWS, S)
    sibling_rows = groups.reshape(N_GRP // 2, 2, GROUP_ROWS, S)[:, ::-1].reshape(N_GRP, GROUP_ROWS, S)
    stacked = jnp.concatenate([groups, sibling_rows], axis=1)
    far_blocks = far_coupling.reshape(N_GRP, N_NODE * M, 2 * GROUP_ROWS)

    def product(operands):
        return jnp.dot(operands[0], operands[1], preferred_element_type=jnp.float32).astype(jnp.bfloat16)

    far_field = lax.map(product, (far_blocks, stacked)).reshape(N, S)
    return parent_rows, transfer, far_field
```

```python
import jax
import jax.numpy as jnp
from jax import lax
from jax.experimental import pallas as pl
from jax.experimental.pallas import tpu as pltpu
from jax.sharding import PartitionSpec as P

NZ, NY = 8, 4
F32, BF16 = jnp.float32, jnp.bfloat16
VMEM = pl.BlockSpec(memory_space=pltpu.VMEM)


def moved(block, where):
    route = []
    for z in range(NZ):
        for y in range(NY):
            to_z, to_y = where(z, y)
            route.append((z * NY + y, (to_z % NZ) * NY + to_y % NY))
    return lax.ppermute(block, "node", route)


def other_core(block):
    return lax.ppermute(block, "grp", [(g, g ^ 1) for g in range(lax.axis_size("grp"))])


def dot(a, b):
    return jnp.dot(a, b, preferred_element_type=F32)


def dot_t(a, b):
    return lax.dot_general(a, b, (((0,), (0,)), ((), ())), preferred_element_type=F32)


def chosen_rows(parent_pivots, position):
    slots, count = parent_pivots.shape
    at = lax.broadcasted_iota(jnp.int32, (slots, count), 0) == position // 2
    pivots = jnp.sum(jnp.where(at, parent_pivots[...], 0), axis=0, keepdims=True)
    second = (pivots >= count).astype(jnp.int32)
    return pivots - second * count, second == position % 2


def one_hot_columns(rows, keep, size):
    at = lax.broadcasted_iota(jnp.int32, (size, rows.shape[1]), 0) == rows
    return jnp.where(at & keep, 1.0, 0.0).astype(BF16)


def leaf_kernel(samples, omega, diag, leaf_pivots, interp, parent_pivots, skel, comp):
    position = lax.axis_index("node")
    rows, mine = chosen_rows(parent_pivots, position)
    rank = rows.shape[1]
    pivots = leaf_pivots[...]
    leaf_pick = one_hot_columns(pivots, pivots >= 0, samples.shape[0])
    pick = dot(leaf_pick, one_hot_columns(rows, mine, rank)).astype(BF16)
    w = omega[...]
    comp[...] = dot_t(interp[...], w).astype(BF16)
    diag_rows = dot_t(pick, diag[...]).astype(BF16)
    skel[...] = (dot_t(pick, samples[...]) - dot(diag_rows, w)).astype(BF16)


def share_kernel(parent_pivots, coupling_sib, skel, comp, wide, narrow):
    position = lax.axis_index("node")
    rows, mine = chosen_rows(parent_pivots, position)
    pick = one_hot_columns(rows, jnp.logical_not(mine), rows.shape[1])
    coupling_rows = dot_t(pick, coupling_sib[...]).astype(BF16)
    share = skel[...].astype(F32) - dot(coupling_rows, comp[...])
    wide[...] = share
    narrow[...] = share.astype(BF16)


def join_kernel(wide, received, rows, half):
    joined = (wide[...] + received[...].astype(F32)).astype(BF16)
    rows[...] = joined
    n = half.shape[0]
    odd = lax.axis_index("node") % 2
    half[...] = jnp.where(odd == 0, joined[:n], joined[n:])


def stack_kernel(*refs):
    pieces, out = refs[:-1], refs[-1]
    position = lax.axis_index("node")
    z, pair = position // NY, position % NY // 2
    n = pieces[0].shape[0]
    for at, piece in enumerate(pieces):
        step, other = PLACES[at]
        parent = (z + step + NZ) % NZ * 2 + (1 - pair if other else pair)
        out[pl.ds(pl.multiple_of(parent * n, n), n), :] = piece[...]


PLACES = [(0, 0), (0, 1)]
for hop in (1, 2, 3):
    PLACES += [(-hop, 0), (hop, 0), (-hop, 1), (hop, 1)]
PLACES += [(-4, 0), (4, 1)]


def call(kernel, outs, *args):
    return pl.pallas_call(
        kernel,
        out_shape=outs,
        in_specs=[VMEM] * len(args),
        out_specs=jax.tree.map(lambda _: VMEM, outs),
        compiler_params=pltpu.CompilerParams(vmem_limit_bytes=32 << 20),
    )(*args)


def shape(rows, columns, dtype=BF16):
    return jax.ShapeDtypeStruct((rows, columns), dtype)


def shards(
    samples,
    omega,
    diag_block,
    leaf_pivots,
    leaf_interp,
    coupling,
    parent_pivots,
    parent_interp,
    far_coupling,
):
    rank, width = coupling.shape[0], samples.shape[1]
    own_width = far_coupling.shape[1] // 2

    def pair(z, y):
        return z, y ^ 1

    coupling_sib = moved(coupling, pair)
    far_sib = other_core(far_coupling[:, own_width:])
    skel, comp = call(
        leaf_kernel,
        (shape(rank, width), shape(rank, width)),
        samples, omega, diag_block, leaf_pivots, leaf_interp, parent_pivots,
    )
    wide, narrow = call(
        share_kernel,
        (shape(rank, width, F32), shape(rank, width)),
        parent_pivots, coupling_sib, skel, comp,
    )
    received = moved(narrow, pair)
    rows, parent_half = call(
        join_kernel, (shape(rank, width), shape(rank // 2, width)), wide, received
    )
    transfer = dot(leaf_interp, parent_interp).astype(BF16)
    others = moved(rows, lambda z, y: (z, 3 - y))

    def up(block):
        return moved(block, lambda z, y: (z + 1, y))

    def down(block):
        return moved(block, lambda z, y: (z - 1, y))

    pieces = [rows, others]
    a_up = a_down = rows
    b_up = b_down = others
    for _ in range(3):
        a_up, a_down, b_up, b_down = up(a_up), down(a_down), up(b_up), down(b_down)
        pieces += [a_up, a_down, b_up, b_down]
    pieces += [up(a_up), down(b_down)]
    stacked = call(stack_kernel, shape(own_width, width), *pieces)
    for_sib = dot(far_sib, stacked).astype(BF16)
    from_sib = other_core(for_sib)
    far_field = dot(far_coupling[:, :own_width], stacked) + from_sib.astype(F32)
    return (parent_half, transfer, far_field.astype(BF16))


def solution(mesh):
    leaf = P(("grp", "node"), None)
    placed = (leaf, leaf, leaf, leaf, leaf, leaf, P("grp", None), leaf, leaf)
    return jax.shard_map(
        shards, mesh=mesh, in_specs=placed, out_specs=(leaf, leaf, leaf), check_vma=False
    )
```

```python
import jax
import jax.numpy as jnp
from jax import lax
from jax.experimental import pallas as pl
from jax.experimental.pallas import tpu as pltpu
from jax.sharding import PartitionSpec as P

NZ, NY = 8, 4
F32, BF16 = jnp.float32, jnp.bfloat16
VMEM = pl.BlockSpec(memory_space=pltpu.VMEM)


def moved(block, where):
    route = []
    for z in range(NZ):
        for y in range(NY):
            to_z, to_y = where(z, y)
            route.append((z * NY + y, (to_z % NZ) * NY + to_y % NY))
    return lax.ppermute(block, "node", route)


def other_core(block):
    return lax.ppermute(block, "grp", [(g, g ^ 1) for g in range(lax.axis_size("grp"))])


def dot(a, b):
    return jnp.dot(a, b, preferred_element_type=F32)


def dot_t(a, b):
    return lax.dot_general(a, b, (((0,), (0,)), ((), ())), preferred_element_type=F32)


def chosen_rows(parent_pivots, position):
    slots, count = parent_pivots.shape
    at = lax.broadcasted_iota(jnp.int32, (slots, count), 0) == position // 2
    pivots = jnp.sum(jnp.where(at, parent_pivots, 0), axis=0, keepdims=True)
    second = (pivots >= count).astype(jnp.int32)
    return pivots - second * count, second == position % 2


def one_hot_columns(rows, keep, size):
    at = lax.broadcasted_iota(jnp.int32, (size, rows.shape[1]), 0) == rows
    return jnp.where(at & keep, 1.0, 0.0).astype(BF16)


def leaf_kernel(pivots, packed, skel, comp):
    size = packed.shape[0]
    rank = pivots.shape[1]
    width = skel.shape[1]
    samples, omega = packed[:, :width], packed[:, width : 2 * width]
    diag, interp = packed[:, 2 * width : 2 * width + size], packed[:, 2 * width + size :]
    comp[...] = dot_t(interp, omega).astype(BF16)
    position = lax.axis_index("node")
    rows, mine = chosen_rows(pivots[1:, :], position)
    leaf_pivots = pivots[:1, :]
    leaf_pick = one_hot_columns(leaf_pivots, leaf_pivots >= 0, size)
    pick = dot(leaf_pick, one_hot_columns(rows, mine, rank)).astype(BF16)
    diag_rows = dot_t(pick, diag).astype(BF16)
    skel[...] = (dot_t(pick, samples) - dot(diag_rows, omega)).astype(BF16)


def share_kernel(pivots, coupling_sib, skel, comp, wide, narrow):
    position = lax.axis_index("node")
    rows, mine = chosen_rows(pivots[1:, :], position)
    pick = one_hot_columns(rows, jnp.logical_not(mine), rows.shape[1])
    coupling_rows = dot_t(pick, coupling_sib[...]).astype(BF16)
    share = skel[...].astype(F32) - dot(coupling_rows, comp[...])
    wide[...] = share
    narrow[...] = share.astype(BF16)


def join_kernel(wide, received, rows):
    rows[...] = (wide[...] + received[...].astype(F32)).astype(BF16)


def half_kernel(rows, half):
    n = half.shape[0]
    odd = lax.axis_index("node") % 2
    half[...] = jnp.where(odd == 0, rows[:n, :], rows[n:, :])


EARLY, LATE = (0, 1, -1, 2, -2), (3, -3, 4)


def products(hops, far, first, pieces, total):
    position = lax.axis_index("node")
    z, swap = position // NY, position % NY // 2
    n = pieces[0].shape[0]
    for at, hop in enumerate(hops):
        a, b = pieces[2 * at][...], pieces[2 * at + 1][...]
        block = jnp.concatenate([jnp.where(swap == 0, a, b), jnp.where(swap == 0, b, a)], axis=0)
        start = pl.multiple_of(first + (z - hop + NZ) % NZ * 2 * n, 2 * n)
        part = dot(far[:, pl.ds(start, 2 * n)], block)
        total = part if total is None else total + part
    return total


def early_kernel(far, far_sib, *refs):
    pieces, (own, sib) = refs[:-2], refs[-2:]
    sib[...] = products(EARLY, far_sib, far_sib.shape[1] // 2, pieces, None)
    own[...] = products(EARLY, far, 0, pieces, None)


def late_sib_kernel(far_sib, sib, *refs):
    pieces, out = refs[:-1], refs[-1]
    out[...] = products(LATE, far_sib, far_sib.shape[1] // 2, pieces, sib[...]).astype(BF16)


def late_own_kernel(far, own, *refs):
    refs[-1][...] = products(LATE, far, 0, refs[:-1], own[...])


def sum_kernel(own, received, out):
    out[...] = (own[...] + received[...].astype(F32)).astype(BF16)


def call(kernel, outs, *args):
    return pl.pallas_call(
        kernel,
        out_shape=outs,
        in_specs=[VMEM] * len(args),
        out_specs=jax.tree.map(lambda _: VMEM, outs),
        compiler_params=pltpu.CompilerParams(vmem_limit_bytes=24 << 20),
    )(*args)


def shape(rows, columns, dtype=BF16):
    return jax.ShapeDtypeStruct((rows, columns), dtype)


def shards(
    samples,
    omega,
    diag_block,
    leaf_pivots,
    leaf_interp,
    coupling,
    parent_pivots,
    parent_interp,
    far_coupling,
):
    rank, width = coupling.shape[0], samples.shape[1]

    def pair(z, y):
        return z, y ^ 1

    coupling_sib = moved(coupling, pair)
    far_sib = other_core(far_coupling)
    pivots = jnp.concatenate([leaf_pivots, parent_pivots])
    skel, comp = call(
        leaf_kernel,
        (shape(rank, width), shape(rank, width)),
        pivots, jnp.concatenate([samples, omega, diag_block, leaf_interp], axis=1),
    )
    transfer = dot(leaf_interp, parent_interp).astype(BF16)
    wide, narrow = call(
        share_kernel,
        (shape(rank, width, F32), shape(rank, width)),
        pivots, coupling_sib, skel, comp,
    )
    received = moved(narrow, pair)
    rows = call(join_kernel, shape(rank, width), wide, received)
    parent_half = call(half_kernel, shape(rank // 2, width), rows)
    others = moved(rows, lambda z, y: (z, 3 - y))

    def up(block):
        return moved(block, lambda z, y: (z + 1, y))

    def down(block):
        return moved(block, lambda z, y: (z - 1, y))

    pieces = [rows, others]
    a_up = a_down = rows
    b_up = b_down = others
    for _ in range(3):
        a_up, a_down, b_up, b_down = up(a_up), down(a_down), up(b_up), down(b_down)
        pieces += [a_up, b_up, a_down, b_down]
    pieces += [up(a_up), down(b_down)]
    early, late = pieces[: 2 * len(EARLY)], pieces[2 * len(EARLY) :]
    total = shape(far_coupling.shape[0], width, F32)
    own, sib = call(early_kernel, (total, total), far_coupling, far_sib, *early)
    from_sib = other_core(call(late_sib_kernel, shape(*total.shape), far_sib, sib, *late))
    own = call(late_own_kernel, total, far_coupling, own, *late)
    far_field = call(sum_kernel, shape(*total.shape), own, from_sib)
    return (parent_half, transfer, far_field)


def solution(mesh):
    leaf = P(("grp", "node"), None)
    placed = (leaf, leaf, leaf, leaf, leaf, leaf, P("grp", None), leaf, leaf)
    return jax.shard_map(
        shards, mesh=mesh, in_specs=placed, out_specs=(leaf, leaf, leaf), check_vma=False
    )
```

```python
import jax
import jax.numpy as jnp
from jax import lax
from jax.experimental import pallas as pl
from jax.experimental.pallas import tpu as pltpu
from jax.sharding import PartitionSpec as P

NZ, NY = 8, 4
F32, BF16 = jnp.float32, jnp.bfloat16
VMEM = pl.BlockSpec(memory_space=pltpu.VMEM)


def moved(block, where):
    route = []
    for z in range(NZ):
        for y in range(NY):
            to_z, to_y = where(z, y)
            route.append((z * NY + y, (to_z % NZ) * NY + to_y % NY))
    return lax.ppermute(block, "node", route)


def other_core(block):
    return lax.ppermute(block, "grp", [(g, g ^ 1) for g in range(lax.axis_size("grp"))])


def dot(a, b):
    return jnp.dot(a, b, preferred_element_type=F32)


def dot_t(a, b):
    return lax.dot_general(a, b, (((0,), (0,)), ((), ())), preferred_element_type=F32)


def chosen_rows(parent_pivots, position):
    slots, count = parent_pivots.shape
    at = lax.broadcasted_iota(jnp.int32, (slots, count), 0) == position // 2
    pivots = jnp.sum(jnp.where(at, parent_pivots, 0), axis=0, keepdims=True)
    second = (pivots >= count).astype(jnp.int32)
    return pivots - second * count, second == position % 2


def one_hot_columns(rows, keep, size):
    at = lax.broadcasted_iota(jnp.int32, (size, rows.shape[1]), 0) == rows
    return jnp.where(at & keep, 1.0, 0.0).astype(BF16)


def leaf_kernel(pivots, packed, skel, comp):
    size = packed.shape[0]
    rank = pivots.shape[1]
    width = skel.shape[1]
    samples, omega = packed[:, :width], packed[:, width : 2 * width]
    diag, interp = packed[:, 2 * width : 2 * width + size], packed[:, 2 * width + size :]
    comp[...] = dot_t(interp, omega).astype(BF16)
    position = lax.axis_index("node")
    rows, mine = chosen_rows(pivots[1:, :], position)
    leaf_pivots = pivots[:1, :]
    leaf_pick = one_hot_columns(leaf_pivots, leaf_pivots >= 0, size)
    pick = dot(leaf_pick, one_hot_columns(rows, mine, rank)).astype(BF16)
    diag_rows = dot_t(pick, diag).astype(BF16)
    skel[...] = (dot_t(pick, samples) - dot(diag_rows, omega)).astype(BF16)


def share_kernel(pivots, coupling_sib, skel, comp, wide, narrow):
    position = lax.axis_index("node")
    rows, mine = chosen_rows(pivots[1:, :], position)
    pick = one_hot_columns(rows, jnp.logical_not(mine), rows.shape[1])
    coupling_rows = dot_t(pick, coupling_sib[...]).astype(BF16)
    share = skel[...].astype(F32) - dot(coupling_rows, comp[...])
    wide[...] = share
    narrow[...] = share.astype(BF16)


def join_kernel(wide, received, rows):
    rows[...] = (wide[...] + received[...].astype(F32)).astype(BF16)


def half_kernel(rows, half):
    n = half.shape[0]
    odd = lax.axis_index("node") % 2
    half[...] = jnp.where(odd == 0, rows[:n, :], rows[n:, :])


EARLY, MIDDLE, LATE = (0, 1, -1, 2, -2), (-3, 4), (3,)


def products(hops, far, first, pieces, total):
    position = lax.axis_index("node")
    z, swap = position // NY, position % NY // 2
    n = pieces[0].shape[0]
    for at, hop in enumerate(hops):
        a, b = pieces[2 * at][...], pieces[2 * at + 1][...]
        block = jnp.concatenate([jnp.where(swap == 0, a, b), jnp.where(swap == 0, b, a)], axis=0)
        start = pl.multiple_of(first + (z - hop + NZ) % NZ * 2 * n, 2 * n)
        part = dot(far[:, pl.ds(start, 2 * n)], block)
        total = part if total is None else total + part
    return total


def early_kernel(far, far_sib, *refs):
    pieces, (own, sib) = refs[:-2], refs[-2:]
    sib[...] = products(EARLY, far_sib, far_sib.shape[1] // 2, pieces, None)
    own[...] = products(EARLY, far, 0, pieces, None)


def middle_kernel(far, far_sib, own_in, sib_in, *refs):
    pieces, (own, sib) = refs[:-2], refs[-2:]
    sib[...] = products(MIDDLE, far_sib, far_sib.shape[1] // 2, pieces, sib_in[...])
    own[...] = products(MIDDLE, far, 0, pieces, own_in[...])


def late_sib_kernel(far_sib, sib, *refs):
    pieces, out = refs[:-1], refs[-1]
    out[...] = products(LATE, far_sib, far_sib.shape[1] // 2, pieces, sib[...]).astype(BF16)


def late_own_kernel(far, own, *refs):
    refs[-1][...] = products(LATE, far, 0, refs[:-1], own[...])


def sum_kernel(own, received, out):
    out[...] = (own[...] + received[...].astype(F32)).astype(BF16)


def call(kernel, outs, *args):
    return pl.pallas_call(
        kernel,
        out_shape=outs,
        in_specs=[VMEM] * len(args),
        out_specs=jax.tree.map(lambda _: VMEM, outs),
        compiler_params=pltpu.CompilerParams(vmem_limit_bytes=24 << 20),
    )(*args)


def shape(rows, columns, dtype=BF16):
    return jax.ShapeDtypeStruct((rows, columns), dtype)


def shards(
    samples,
    omega,
    diag_block,
    leaf_pivots,
    leaf_interp,
    coupling,
    parent_pivots,
    parent_interp,
    far_coupling,
):
    rank, width = coupling.shape[0], samples.shape[1]

    def pair(z, y):
        return z, y ^ 1

    coupling_sib = moved(coupling, pair)
    far_sib = other_core(far_coupling)
    pivots = jnp.concatenate([leaf_pivots, parent_pivots])
    skel, comp = call(
        leaf_kernel,
        (shape(rank, width), shape(rank, width)),
        pivots, jnp.concatenate([samples, omega, diag_block, leaf_interp], axis=1),
    )
    transfer = dot(leaf_interp, parent_interp).astype(BF16)
    wide, narrow = call(
        share_kernel,
        (shape(rank, width, F32), shape(rank, width)),
        pivots, coupling_sib, skel, comp,
    )
    received = moved(narrow, pair)
    rows = call(join_kernel, shape(rank, width), wide, received)
    parent_half = call(half_kernel, shape(rank // 2, width), rows)
    others = moved(rows, lambda z, y: (z, 3 - y))

    def up(block):
        return moved(block, lambda z, y: (z + 1, y))

    def down(block):
        return moved(block, lambda z, y: (z - 1, y))

    pieces = [rows, others]
    a_up, a_down = up(rows), down(rows)
    b_up = up(others)
    b_down = moved(rows, lambda z, y: (z - 1, 3 - y))
    pieces += [a_up, b_up, a_down, b_down]
    for _ in range(2):
        a_up, a_down, b_up, b_down = up(a_up), down(a_down), up(b_up), down(b_down)
        pieces += [a_up, b_up, a_down, b_down]
    pieces += [up(a_up), down(b_down)]
    early, third, middle = pieces[:10], pieces[10:12], pieces[12:]
    total = shape(far_coupling.shape[0], width, F32)
    own, sib = call(early_kernel, (total, total), far_coupling, far_sib, *early)
    own, sib = call(middle_kernel, (total, total), far_coupling, far_sib, own, sib, *middle)
    from_sib = other_core(call(late_sib_kernel, shape(*total.shape), far_sib, sib, *third))
    own = call(late_own_kernel, total, far_coupling, own, *third)
    far_field = call(sum_kernel, shape(*total.shape), own, from_sib)
    return (parent_half, transfer, far_field)


def solution(mesh):
    leaf = P(("grp", "node"), None)
    placed = (leaf, leaf, leaf, leaf, leaf, leaf, P("grp", None), leaf, leaf)
    return jax.shard_map(
        shards, mesh=mesh, in_specs=placed, out_specs=(leaf, leaf, leaf), check_vma=False
    )
```

```python
import jax
import jax.numpy as jnp
from jax import lax
from jax.experimental import pallas as pl
from jax.experimental.pallas import tpu as pltpu
from jax.sharding import PartitionSpec as P

NZ, NY = 8, 4
F32, BF16 = jnp.float32, jnp.bfloat16
VMEM = pl.BlockSpec(memory_space=pltpu.VMEM)


def moved(block, where):
    route = []
    for z in range(NZ):
        for y in range(NY):
            to_z, to_y = where(z, y)
            route.append((z * NY + y, (to_z % NZ) * NY + to_y % NY))
    return lax.ppermute(block, "node", route)


def other_core(block):
    return lax.ppermute(block, "grp", [(g, g ^ 1) for g in range(lax.axis_size("grp"))])


def dot(a, b):
    return jnp.dot(a, b, preferred_element_type=F32)


def dot_t(a, b):
    return lax.dot_general(a, b, (((0,), (0,)), ((), ())), preferred_element_type=F32)


def chosen_rows(parent_pivots, position):
    slots, count = parent_pivots.shape
    at = lax.broadcasted_iota(jnp.int32, (slots, count), 0) == position // 2
    pivots = jnp.sum(jnp.where(at, parent_pivots, 0), axis=0, keepdims=True)
    second = (pivots >= count).astype(jnp.int32)
    return pivots - second * count, second == position % 2


def one_hot_columns(rows, keep, size):
    at = lax.broadcasted_iota(jnp.int32, (size, rows.shape[1]), 0) == rows
    return jnp.where(at & keep, 1.0, 0.0).astype(BF16)


def leaf_kernel(leaf_pivots, parent_pivots, packed, skel, comp):
    size = packed.shape[0]
    rank, width = skel.shape
    samples, omega = packed[:, :width], packed[:, width : 2 * width]
    diag, interp = packed[:, 2 * width : 2 * width + size], packed[:, 2 * width + size :]
    comp[...] = dot_t(interp, omega).astype(BF16)
    position = lax.axis_index("node")
    rows, mine = chosen_rows(parent_pivots[...], position)
    leaf_pivots = leaf_pivots[...]
    leaf_pick = one_hot_columns(leaf_pivots, leaf_pivots >= 0, size)
    pick = dot(leaf_pick, one_hot_columns(rows, mine, rank)).astype(BF16)
    diag_rows = dot_t(pick, diag).astype(BF16)
    skel[...] = (dot_t(pick, samples) - dot(diag_rows, omega)).astype(BF16)


def share_kernel(parent_pivots, coupling_sib, skel, comp, wide, narrow):
    position = lax.axis_index("node")
    rows, mine = chosen_rows(parent_pivots[...], position)
    pick = one_hot_columns(rows, jnp.logical_not(mine), rows.shape[1])
    coupling_rows = dot_t(pick, coupling_sib[...]).astype(BF16)
    share = skel[...].astype(F32) - dot(coupling_rows, comp[...])
    wide[...] = share
    narrow[...] = share.astype(BF16)


def join_kernel(wide, received, rows):
    rows[...] = (wide[...] + received[...].astype(F32)).astype(BF16)


def half_kernel(rows, half):
    n = half.shape[0]
    odd = lax.axis_index("node") % 2
    half[...] = jnp.where(odd == 0, rows[:n, :], rows[n:, :])


EARLY, MIDDLE, LATE = (0, 1, -1, 2, -2), (-3, 4), (3,)


def products(hops, far, first, pieces, total):
    position = lax.axis_index("node")
    z, swap = position // NY, position % NY // 2
    n = pieces[0].shape[0]
    for at, hop in enumerate(hops):
        a, b = pieces[2 * at][...], pieces[2 * at + 1][...]
        block = jnp.concatenate([jnp.where(swap == 0, a, b), jnp.where(swap == 0, b, a)], axis=0)
        start = pl.multiple_of(first + (z - hop + NZ) % NZ * 2 * n, 2 * n)
        part = dot(far[:, pl.ds(start, 2 * n)], block)
        total = part if total is None else total + part
    return total


def early_kernel(far, far_sib, *refs):
    pieces, (own, sib) = refs[:-2], refs[-2:]
    sib[...] = products(EARLY, far_sib, far_sib.shape[1] // 2, pieces, None)
    own[...] = products(EARLY, far, 0, pieces, None)


def middle_kernel(far, far_sib, own_in, sib_in, *refs):
    pieces, (own, sib) = refs[:-2], refs[-2:]
    sib[...] = products(MIDDLE, far_sib, far_sib.shape[1] // 2, pieces, sib_in[...])
    own[...] = products(MIDDLE, far, 0, pieces, own_in[...])


def late_sib_kernel(far_sib, sib, *refs):
    pieces, out = refs[:-1], refs[-1]
    out[...] = products(LATE, far_sib, far_sib.shape[1] // 2, pieces, sib[...]).astype(BF16)


def late_own_kernel(far, own, *refs):
    refs[-1][...] = products(LATE, far, 0, refs[:-1], own[...])


def sum_kernel(own, received, out):
    out[...] = (own[...] + received[...].astype(F32)).astype(BF16)


def call(kernel, outs, *args):
    return pl.pallas_call(
        kernel,
        out_shape=outs,
        in_specs=[VMEM] * len(args),
        out_specs=jax.tree.map(lambda _: VMEM, outs),
        compiler_params=pltpu.CompilerParams(vmem_limit_bytes=24 << 20),
    )(*args)


def shape(rows, columns, dtype=BF16):
    return jax.ShapeDtypeStruct((rows, columns), dtype)


def shards(
    samples,
    omega,
    diag_block,
    leaf_pivots,
    leaf_interp,
    coupling,
    parent_pivots,
    parent_interp,
    far_coupling,
):
    rank, width = coupling.shape[0], samples.shape[1]

    def pair(z, y):
        return z, y ^ 1

    coupling_sib = moved(coupling, pair)
    skel, comp = call(
        leaf_kernel,
        (shape(rank, width), shape(rank, width)),
        leaf_pivots, parent_pivots, jnp.concatenate([samples, omega, diag_block, leaf_interp], axis=1),
    )
    far_coupling, coupling_sib = lax.optimization_barrier((far_coupling, coupling_sib))
    far_sib = other_core(far_coupling)
    transfer = dot(leaf_interp, parent_interp).astype(BF16)
    wide, narrow = call(
        share_kernel,
        (shape(rank, width, F32), shape(rank, width)),
        parent_pivots, coupling_sib, skel, comp,
    )
    received = moved(narrow, pair)
    rows = call(join_kernel, shape(rank, width), wide, received)
    parent_half = call(half_kernel, shape(rank // 2, width), rows)
    others = moved(rows, lambda z, y: (z, 3 - y))

    def up(block):
        return moved(block, lambda z, y: (z + 1, y))

    def down(block):
        return moved(block, lambda z, y: (z - 1, y))

    pieces = [rows, others]
    a_up, a_down = up(rows), down(rows)
    b_up = up(others)
    b_down = moved(rows, lambda z, y: (z - 1, 3 - y))
    pieces += [a_up, b_up, a_down, b_down]
    for _ in range(2):
        a_up, a_down, b_up, b_down = up(a_up), down(a_down), up(b_up), down(b_down)
        pieces += [a_up, b_up, a_down, b_down]
    pieces += [up(a_up), down(b_down)]
    early, third, middle = pieces[:10], pieces[10:12], pieces[12:]
    total = shape(far_coupling.shape[0], width, F32)
    own, sib = call(early_kernel, (total, total), far_coupling, far_sib, *early)
    own, sib = call(middle_kernel, (total, total), far_coupling, far_sib, own, sib, *middle)
    from_sib = other_core(call(late_sib_kernel, shape(*total.shape), far_sib, sib, *third))
    own = call(late_own_kernel, total, far_coupling, own, *third)
    far_field = call(sum_kernel, shape(*total.shape), own, from_sib)
    return (parent_half, transfer, far_field)


def solution(mesh):
    leaf = P(("grp", "node"), None)
    placed = (leaf, leaf, leaf, leaf, leaf, leaf, P("grp", None), leaf, leaf)
    return jax.shard_map(
        shards, mesh=mesh, in_specs=placed, out_specs=(leaf, leaf, leaf), check_vma=False
    )
```
